256 devices in a mesh: row: 16 (over z, x_hi), col: 16 (over y, x_lo, core).
Axes of the slice: x: 4 (x_hi: 2, x_lo: 2; x = x_hi * 2 + x_lo), y: 4, z: 8, core: 2. Of those that a mesh axis runs over, the one named last changes fastest.
Arguments:
- inverse_rows: float32 [1024, 16384], P('row', 'col'), as said below
- tile_mask: int32 [256, 256], replicated, may hold values from 0 to 1, as said below
Outputs:
- covariance: float32 [16384, 16384], P('row', 'col')
The draws below stay inside these ranges and needn't reach their ends.
Inputs may be any that keep to these rules, and one draw needn't show every extreme that they name: inverse_rows[k, i] is 0 where i > 15360 + k; its magnitudes stay below 8 * 1024**-0.25. tile_mask is 0 above the diagonal and 1 on it.
All inputs are finite; a program needn't handle non-finite values.
Results may differ from the reference program's by a relative error of at most 0.000088.
Values sent between devices are 32-bit elements; how exact they have to be, the bound alone decides.
No kernel may reach another device: no remote copies, remote signals or barrier semaphores. Data moves between devices by JAX's collectives and lax.ppermute only.
A program may use at most 128 MiB of HBM per device.

```python
import jax
import jax.numpy as jnp
from jax import lax

N = 16384
KS = 1024
MT = 64


def draw_inverse_rows(key, part):
    key = jax.random.fold_in(key, 11)
    first_key = jax.random.fold_in(key, 0)
    magnitude = KS ** (-0.25)
    values = jax.random.truncated_normal(first_key, -6.0, 6.0, (KS, N), jnp.float32)
    row_ids = jnp.arange(KS, dtype=jnp.int32)[:, None]
    col_ids = jnp.arange(N, dtype=jnp.int32)[None, :]
    return jnp.where(col_ids <= N - KS + row_ids, values * magnitude, 0.0).astype(jnp.float32)


def draw_tile_mask(key, part):
    key = jax.random.fold_in(key, 12)
    tile_count = N // MT
    picks = jax.random.randint(key, (tile_count, tile_count), 0, 4)
    row_ids = jnp.arange(tile_count, dtype=jnp.int32)[:, None]
    col_ids = jnp.arange(tile_count, dtype=jnp.int32)[None, :]
    lower = jnp.where(col_ids < row_ids, (picks < 3).astype(jnp.int32), 0)
    return (lower + (col_ids == row_ids).astype(jnp.int32)).astype(jnp.int32)


def setup_inputs(seed: int = 0) -> dict:
    splits = jax.random.split(jax.random.key(seed), 3)
    inverse_rows = draw_inverse_rows(jax.random.fold_in(splits[2], 71), 0)
    tile_mask = draw_tile_mask(jax.random.fold_in(splits[2], 71), 0)
    return {"inverse_rows": inverse_rows, "tile_mask": tile_mask}


def reference(inverse_rows, tile_mask):
    products = lax.dot_general(inverse_rows, inverse_rows, (((0,), (0,)), ((), ())), precision=lax.Precision.HIGHEST, preferred_element_type=jnp.float32)
    tile_count = N // MT
    shaped = products.reshape(tile_count, MT, tile_count, MT) * tile_mask.astype(jnp.float32)[:, None, :, None]
    return shaped.reshape(N, N)
```

```python
import jax
import jax.numpy as jnp
from jax import lax
from jax.experimental import pallas as pl
from jax.experimental.pallas import tpu as pltpu
from jax.sharding import PartitionSpec as P

MT = 64
AXES = ("row", "col")
NZ = 8
NM = 8
STRIPE = 256


def permute(value, move):
    pairs = []
    for row in range(2 * NZ):
        for col in range(2 * NM):
            xh, m, z, core = move(row % 2, col // 2, row // 2, col % 2)
            pairs.append(
                (row * 2 * NM + col, (z % NZ * 2 + xh) * 2 * NM + m % NM * 2 + core)
            )
    return lax.ppermute(value, AXES, pairs)


def up_z(xh, m, z, core):
    return xh, m, z + 1, core


def down_z(xh, m, z, core):
    return xh, m, z - 1, core


def up_y(xh, m, z, core):
    return xh, m + 2, z, core


def down_y(xh, m, z, core):
    return xh, m - 2, z, core


def other_core(xh, m, z, core):
    return xh, m, z, 1 - core


def ring(block):
    half = block.shape[0] // 2
    p1 = permute(block, up_z)
    m1 = permute(block, down_z)
    p2 = permute(p1, up_z)
    m2 = permute(m1, down_z)
    p3 = permute(p2, up_z)
    m3 = permute(m2, down_z)
    p4 = permute(p3[:half], up_z)
    m4 = permute(m3[half:], down_z)
    return [block, p1, m1, p2, m2, p3, m3, p4, m4]


RING_SHIFT = (0, -1, 1, -2, 2, -3, 3, 4, 4)


def kernel(where, mask_ref, *refs):
    n_right, n_left = 18, 8
    right_in = refs[:n_right]
    left_in = refs[n_right : n_right + n_left]
    out_ref = refs[n_right + n_left]
    left, right, right_hi, right_lo, product, sems, out_sems = refs[n_right + n_left + 1 :]
    z, xh, m, core = where[0], where[1], where[2], where[3]
    active = where[4]
    rows = 64

    copies = []

    def fetch(src, lo, count, buf, slot, offset):
        start = pl.multiple_of(slot * rows + offset, 8)
        copies.append(
            pltpu.make_async_copy(
                src.at[pl.ds(lo, count)], buf.at[pl.ds(start, count)], sems.at[len(copies)]
            )
        )

    def slot_of(zz, x_hi):
        return lax.rem(zz + 2 * NZ, NZ) * 2 + x_hi

    for chain in range(2):
        x_hi = xh if chain == 0 else 1 - xh
        for step in range(9):
            src = right_in[chain * 9 + step]
            slot = slot_of(z + RING_SHIFT[step], x_hi)
            count = src.shape[0]
            fetch(src, 0, count, right, slot, 32 if step == 8 else 0)
    m_other = m + 1 - 2 * lax.rem(m, 2)

    def line_slot(line, kappa):
        return slot_of(lax.rem(line + 2 * NM, NM) - z, kappa)

    pair = (m, m_other)
    layout = [
        (0, 0, pair[0], core), (0, 64, pair[1], core),
        (1, 0, pair[0] - 2, core), (1, 64, pair[1] - 2, core),
        (2, 0, pair[0] + 2, core), (2, 64, pair[1] + 2, core),
        (3, 0, pair[0] + 4, core), (4, 0, pair[1] + 4, core),
        (5, 0, pair[0], 1 - core), (5, 64, pair[1], 1 - core),
        (6, 0, pair[0] - 2, 1 - core), (6, 64, pair[1] - 2, 1 - core),
        (6, 128, pair[0] + 2, 1 - core), (6, 192, pair[1] + 2, 1 - core),
        (7, 0, pair[0] + 4, 1 - core), (7, 64, pair[1] + 4, 1 - core),
    ]
    for array, lo, line, kappa in layout:
        fetch(left_in[array], lo, rows, left, line_slot(line, kappa), 0)
    n_stripes = out_ref.shape[0] // STRIPE

    def store(i):
        return pltpu.make_async_copy(
            product.at[i], out_ref.at[pl.ds(i * STRIPE, STRIPE)], out_sems.at[i]
        )

    @pl.when(active == 0)
    def _():
        for i in range(n_stripes):
            product[i] = jnp.zeros_like(product[i])
            store(i).start()

    @pl.when(active != 0)
    def _():
        for copy in copies:
            copy.start()
        for copy in copies:
            copy.wait()
        full = right[...]
        high = full.astype(jnp.bfloat16)
        right_hi[...] = high
        right_lo[...] = (full - high.astype(jnp.float32)).astype(jnp.bfloat16)
        for i in range(n_stripes):
            part = left[:, i * STRIPE : (i + 1) * STRIPE]
            part_hi = part.astype(jnp.bfloat16)
            part_lo = (part - part_hi.astype(jnp.float32)).astype(jnp.bfloat16)

            def dot(a, b):
                return lax.dot_general(
                    a, b, (((0,), (0,)), ((), ())), preferred_element_type=jnp.float32
                )

            total = (
                dot(part_hi, right_lo[...]) + dot(part_lo, right_hi[...])
            ) + dot(part_hi, right_hi[...])
            for t in range(STRIPE // MT):
                tile = i * (STRIPE // MT) + t
                product[i, t * MT : (t + 1) * MT, :] = (
                    total[t * MT : (t + 1) * MT] * mask_ref[tile : tile + 1, :]
                )
            store(i).start()

    for i in range(n_stripes):
        store(i).wait()


def local(inverse_rows, tile_mask):
    row = lax.axis_index("row")
    col = lax.axis_index("col")
    z, xh = row // 2, row % 2
    m, core = col // 2, col % 2
    cols = inverse_rows.shape[1]
    n_tiles = cols // MT

    spread = permute(inverse_rows, lambda xh, m, z, core: (core, m + z, z, xh))
    mine = permute(spread, lambda xh, m, z, core: (xh, m, m - z, core))
    beside = permute(mine, lambda xh, m, z, core: (xh, m ^ 1, z, core))
    both = jnp.concatenate([mine, beside])
    y1 = permute(both, up_y)
    y3 = permute(both, down_y)
    y2a = permute(y1[:64], up_y)
    y2b = permute(y3[64:], down_y)
    c0 = permute(both, other_core)
    c1 = permute(jnp.concatenate([y1, y3]), other_core)
    c2 = permute(jnp.concatenate([y2a, y2b]), other_core)
    left = [both, y1, y3, y2a, y2b, c0, c1, c2]

    partner = permute(inverse_rows, lambda xh, m, z, core: (1 - xh, m, z, core))
    right = ring(inverse_rows) + ring(partner)

    block = lax.dynamic_slice(tile_mask, (row * n_tiles, col * n_tiles), (n_tiles, n_tiles))
    mask = jnp.broadcast_to(block[:, :, None], (n_tiles, n_tiles, MT)).reshape(n_tiles, cols)
    where = jnp.stack([z, xh, m, core, (row >= col).astype(jnp.int32)]).astype(jnp.int32)
    any_spec = pl.BlockSpec(memory_space=pl.ANY)
    depth = 1024
    return pl.pallas_call(
        kernel,
        out_shape=jax.ShapeDtypeStruct((cols, cols), jnp.float32),
        in_specs=[
            pl.BlockSpec(memory_space=pltpu.SMEM),
            pl.BlockSpec(memory_space=pltpu.VMEM),
        ]
        + [any_spec] * (len(right) + len(left)),
        out_specs=any_spec,
        scratch_shapes=[
            pltpu.VMEM((depth, cols), jnp.float32),
            pltpu.VMEM((depth, cols), jnp.float32),
            pltpu.VMEM((depth, cols), jnp.bfloat16),
            pltpu.VMEM((depth, cols), jnp.bfloat16),
            pltpu.VMEM((cols // STRIPE, STRIPE, cols), jnp.float32),
            pltpu.SemaphoreType.DMA((len(right) + 16,)),
            pltpu.SemaphoreType.DMA((cols // STRIPE,)),
        ],
        compiler_params=pltpu.CompilerParams(vmem_limit_bytes=40 * 1024 * 1024),
    )(where, mask.astype(jnp.float32), *right, *left)


def solution(mesh):
    return jax.shard_map(
        local,
        mesh=mesh,
        in_specs=(P("row", "col"), P()),
        out_specs=P("row", "col"),
        check_vma=False,
    )
```

```python
import functools

import jax
import jax.numpy as jnp
from jax import lax
from jax.experimental import pallas as pl
from jax.experimental.pallas import tpu as pltpu
from jax.sharding import PartitionSpec as P

MT = 64
AXES = ("row", "col")
NZ = 8
NM = 8
STRIPE = 256
WINDOW = 4


def permute(value, move):
    pairs = []
    for row in range(2 * NZ):
        for col in range(2 * NM):
            xh, m, z, core = move(row % 2, col // 2, row // 2, col % 2)
            pairs.append(
                (row * 2 * NM + col, (z % NZ * 2 + xh) * 2 * NM + m % NM * 2 + core)
            )
    return lax.ppermute(value, AXES, pairs)


def along_z(value):
    return permute(value, lambda xh, m, z, core: (xh, m, z + 1 - 2 * core, core))


def along_z_across(value):
    return permute(value, lambda xh, m, z, core: (1 - xh, m, z + 1 - 2 * core, core))


def along_y(value):
    return permute(value, lambda xh, m, z, core: (xh, m + 2 - 4 * core, z, core))


def into_plane(value):
    return permute(value, lambda xh, m, z, core: (core, m + z + 4 * xh, z, xh))


def to_rows(value):
    return permute(value, lambda xh, m, z, core: (xh, m, m - z + 4 * core, core))


def other_core(value):
    return permute(value, lambda xh, m, z, core: (xh, m, z, 1 - core))


def other_xh(value):
    return permute(value, lambda xh, m, z, core: (1 - xh, m, z, core))


def other_xl(value):
    return permute(value, lambda xh, m, z, core: (xh, m ^ 1, z, core))


class Steps:
    def __init__(self, window):
        self.window = window
        self.results = []

    def __call__(self, move, value):
        if len(self.results) >= self.window:
            value, _ = lax.optimization_barrier((value, self.results[-self.window]))
        self.results.append(move(value))
        return self.results[-1]


def after(value, *others):
    return lax.optimization_barrier((value, *others))[0]


class Pieces:
    def __init__(self):
        self.arrays = []
        self.moves = []

    def add(self, array, *moves):
        index = len(self.arrays)
        self.arrays.append(array)
        self.moves += [(index, *move) for move in moves]


def kernel(moves, n_in, where, mask_in, *refs):
    ins = refs[:n_in]
    out_ref = refs[n_in]
    left, right, left_hi, left_lo, right_hi, right_lo, product, mask, mask_rows, sems, mask_sem, out_sems = refs[
        n_in + 1 :
    ]
    z, xh, m, core = where[0], where[1], where[2], where[3]
    row = z * 2 + xh
    col = m * 2 + core
    sign = 1 - 2 * core
    cols = right_hi.shape[1]
    n_tiles = cols // MT
    all_tiles = mask_in.shape[0]

    def right_slot(key):
        steps, flip = key
        zz = lax.rem(z - sign * steps + 2 * NZ, NZ)
        return zz * 2 + (1 - xh if flip else xh)

    def left_slot(key):
        line, swap = key
        kappa = 1 - core if swap else core
        return lax.rem(line - z + 4 * kappa + NZ, NZ) * 2 + kappa

    copies = {"right": [], "left": []}
    for panel, index, first, count, key, offset in moves:
        buf, slot = (right, right_slot(key)) if panel == "right" else (left, left_slot(key))
        start = pl.multiple_of(slot * 64 + offset, 8)
        total = len(copies["right"]) + len(copies["left"])
        copies[panel].append(
            pltpu.make_async_copy(
                ins[index].at[pl.ds(first, count)], buf.at[pl.ds(start, count)], sems.at[total]
            )
        )
    n_stripes = out_ref.shape[0] // STRIPE

    def store(i):
        return pltpu.make_async_copy(
            product.at[i], out_ref.at[pl.ds(i * STRIPE, STRIPE)], out_sems.at[i]
        )

    @pl.when(row < col)
    def _():
        for i in range(n_stripes):
            product[i] = jnp.zeros_like(product[i])
            store(i).start()

    mask_copy = pltpu.make_async_copy(
        mask_in.at[pl.ds(pl.multiple_of(row * n_tiles, 8), n_tiles)], mask_rows, mask_sem
    )

    @pl.when(row >= col)
    def _():
        mask_copy.start()
        for copy in copies["right"] + copies["left"]:
            copy.start()
        tile = lax.broadcasted_iota(jnp.int32, (all_tiles, cols), 0)
        wanted = col * n_tiles + lax.broadcasted_iota(jnp.int32, (all_tiles, cols), 1) // MT
        pick = (tile == wanted).astype(jnp.bfloat16)
        mask_copy.wait()
        mask[...] = jnp.dot(
            mask_rows[...].astype(jnp.float32).astype(jnp.bfloat16),
            pick,
            preferred_element_type=jnp.float32,
        )

        for panel, full, high, low in (
            ("right", right, right_hi, right_lo),
            ("left", left, left_hi, left_lo),
        ):
            for copy in copies[panel]:
                copy.wait()
            rounded = full[...].astype(jnp.bfloat16)
            high[...] = rounded
            low[...] = (full[...] - rounded.astype(jnp.float32)).astype(jnp.bfloat16)

        def dot(a, b):
            return lax.dot_general(
                a, b, (((0,), (0,)), ((), ())), preferred_element_type=jnp.float32
            )

        for i in range(n_stripes):
            part = slice(i * STRIPE, (i + 1) * STRIPE)
            total = (
                dot(left_hi[:, part], right_lo[...]) + dot(left_lo[:, part], right_hi[...])
            ) + dot(left_hi[:, part], right_hi[...])
            for t in range(STRIPE // MT):
                tile = i * (STRIPE // MT) + t
                product[i, t * MT : (t + 1) * MT, :] = (
                    total[t * MT : (t + 1) * MT] * mask[tile : tile + 1, :]
                )
            store(i).start()

    for i in range(n_stripes):
        store(i).wait()


def local(inverse_rows, tile_mask):
    row = lax.axis_index("row")
    col = lax.axis_index("col")
    z, xh = row // 2, row % 2
    m, core = col // 2, col % 2
    cols = inverse_rows.shape[1]
    n = inverse_rows.shape[0]
    depth = n * 2 * NZ
    cat = lambda *parts: jnp.concatenate(parts)

    own = inverse_rows
    spread = into_plane(own)
    own_pair = cat(own, other_core(after(own, own)))
    a1 = along_z(own_pair)
    partner = other_xh(after(own, own))
    mine = to_rows(spread)
    a2 = along_z(after(a1, a1))
    b1 = other_xh(after(a1, a1))
    copies = jnp.broadcast_to(after(mine, mine)[None], (NM, n, cols))
    groups = [[2 * line + k for line in range(NM)] for k in range(2)]
    lines = lax.all_to_all(
        copies, "col", split_axis=0, concat_axis=0, tiled=True, axis_index_groups=groups
    ).reshape(NM * n, cols)
    a1x = other_core(a1)
    b1x = other_core(b1)
    b2 = along_z(after(b1, a2, a1x))
    a3 = along_z(after(a2, a2))
    a2x = other_core(a2)
    b2x = other_core(b2)
    a4 = along_z(after(a3, b2, a2x, b1x)[:n])
    b3 = along_z(after(b2, a3, b2x))
    b4 = along_z(after(b3, a4)[:n])
    a3x = other_core(a3)
    b3x = other_core(b3)
    swapped_lines = other_core(after(lines, a4, b3, partner))
    right = Pieces()
    right.add(own, (0, n, (0, 0), 0))
    right.add(partner, (0, n, (0, 1), 0))
    for steps, a, b, ax, bx in ((1, a1, b1, a1x, b1x), (2, a2, b2, a2x, b2x), (3, a3, b3, a3x, b3x)):
        right.add(a, (0, n, (steps, 0), 0))
        right.add(b, (0, n, (steps, 1), 0))
        right.add(ax, (n, n, (-steps, 0), 0))
        right.add(bx, (n, n, (-steps, 1), 0))
    right.add(a4, (0, n, (4, 0), 0))
    right.add(b4, (0, n, (4, 1), 0))

    left = Pieces()
    left.add(lines, *[(line * n, n, (line, 0), 0) for line in range(NM)])
    left.add(swapped_lines, *[(line * n, n, (line, 1), 0) for line in range(NM)])

    moves = [("right", *move) for move in right.moves]
    moves += [("left", move[0] + len(right.arrays), *move[1:]) for move in left.moves]
    arrays = [
        pltpu.with_memory_space_constraint(a, pltpu.HBM) for a in right.arrays + left.arrays
    ]
    where = jnp.stack([z, xh, m, core]).astype(jnp.int32)
    return pl.pallas_call(
        functools.partial(kernel, moves, len(arrays)),
        out_shape=jax.ShapeDtypeStruct((cols, cols), jnp.float32),
        in_specs=[
            pl.BlockSpec(memory_space=pltpu.SMEM),
            pl.BlockSpec(memory_space=pltpu.HBM),
        ]
        + [pl.BlockSpec(memory_space=pltpu.HBM)] * len(arrays),
        out_specs=pl.BlockSpec(memory_space=pltpu.HBM),
        scratch_shapes=[
            pltpu.VMEM((depth, cols), jnp.float32),
            pltpu.VMEM((depth, cols), jnp.float32),
            pltpu.VMEM((depth, cols), jnp.bfloat16),
            pltpu.VMEM((depth, cols), jnp.bfloat16),
            pltpu.VMEM((depth, cols), jnp.bfloat16),
            pltpu.VMEM((depth, cols), jnp.bfloat16),
            pltpu.VMEM((cols // STRIPE, STRIPE, cols), jnp.float32),
            pltpu.VMEM((cols // MT, cols), jnp.float32),
            pltpu.VMEM((cols // MT, tile_mask.shape[1]), jnp.int32),
            pltpu.SemaphoreType.DMA((len(moves),)),
            pltpu.SemaphoreType.DMA,
            pltpu.SemaphoreType.DMA((cols // STRIPE,)),
        ],
        compiler_params=pltpu.CompilerParams(vmem_limit_bytes=32 * 1024 * 1024),
    )(where, pltpu.with_memory_space_constraint(tile_mask, pltpu.HBM), *arrays)


def solution(mesh):
    return jax.shard_map(
        local,
        mesh=mesh,
        in_specs=(P("row", "col"), P()),
        out_specs=P("row", "col"),
        check_vma=False,
    )
```

```python
import functools

import jax
import jax.numpy as jnp
from jax import lax
from jax.experimental import pallas as pl
from jax.experimental.pallas import tpu as pltpu
from jax.sharding import PartitionSpec as P

MT = 64
AXES = ("row", "col")
NZ = 8
NM = 8
STRIPE = 256
WINDOW = 4


def permute(value, move):
    pairs = []
    for row in range(2 * NZ):
        for col in range(2 * NM):
            xh, m, z, core = move(row % 2, col // 2, row // 2, col % 2)
            pairs.append(
                (row * 2 * NM + col, (z % NZ * 2 + xh) * 2 * NM + m % NM * 2 + core)
            )
    return lax.ppermute(value, AXES, pairs)


def along_z(value):
    return permute(value, lambda xh, m, z, core: (xh, m, z + 1 - 2 * core, core))


def along_z_across(value):
    return permute(value, lambda xh, m, z, core: (1 - xh, m, z + 1 - 2 * core, core))


def along_y(value):
    return permute(value, lambda xh, m, z, core: (xh, m + 2 - 4 * core, z, core))


def into_plane(value):
    return permute(value, lambda xh, m, z, core: (core, m + z + 4 * xh, z, xh))


def to_rows(value):
    return permute(value, lambda xh, m, z, core: (xh, m, m - z + 4 * core, core))


def other_core(value):
    return permute(value, lambda xh, m, z, core: (xh, m, z, 1 - core))


def other_xh(value):
    return permute(value, lambda xh, m, z, core: (1 - xh, m, z, core))


def other_xl(value):
    return permute(value, lambda xh, m, z, core: (xh, m ^ 1, z, core))


class Steps:
    def __init__(self, window):
        self.window = window
        self.results = []

    def __call__(self, move, value):
        if len(self.results) >= self.window:
            value, _ = lax.optimization_barrier((value, self.results[-self.window]))
        self.results.append(move(value))
        return self.results[-1]


def after(value, *others):
    return lax.optimization_barrier((value, *others))[0]


class Pieces:
    def __init__(self):
        self.arrays = []
        self.moves = []

    def add(self, array, *moves):
        index = len(self.arrays)
        self.arrays.append(array)
        self.moves += [(index, *move) for move in moves]


def kernel(moves, n_in, where, mask_in, *refs):
    ins = refs[:n_in]
    out_ref = refs[n_in]
    left, right, left_hi, left_lo, right_hi, right_lo, product, mask, mask_rows, sems, mask_sem, out_sems = refs[
        n_in + 1 :
    ]
    z, xh, m, core = where[0], where[1], where[2], where[3]
    row = z * 2 + xh
    col = m * 2 + core
    sign = 1 - 2 * core
    cols = right_hi.shape[1]
    n_tiles = cols // MT
    all_tiles = mask_in.shape[0]

    def right_slot(key):
        steps, flip = key
        zz = lax.rem(z - sign * steps + 2 * NZ, NZ)
        return zz * 2 + (1 - xh if flip else xh)

    def left_slot(key):
        line, swap = key
        kappa = 1 - core if swap else core
        return lax.rem(line - z + 4 * kappa + NZ, NZ) * 2 + kappa

    copies = {"right": [], "left": []}
    for panel, index, first, count, key, offset in moves:
        buf, slot = (right, right_slot(key)) if panel == "right" else (left, left_slot(key))
        start = pl.multiple_of(slot * 64 + offset, 8)
        total = len(copies["right"]) + len(copies["left"])
        copies[panel].append(
            pltpu.make_async_copy(
                ins[index].at[pl.ds(first, count)], buf.at[pl.ds(start, count)], sems.at[total]
            )
        )
    n_stripes = out_ref.shape[0] // STRIPE

    def store(i):
        return pltpu.make_async_copy(
            product.at[i], out_ref.at[pl.ds(i * STRIPE, STRIPE)], out_sems.at[i]
        )

    @pl.when(row < col)
    def _():
        for i in range(n_stripes):
            product[i] = jnp.zeros_like(product[i])
            store(i).start()

    mask_copy = pltpu.make_async_copy(
        mask_in.at[pl.ds(pl.multiple_of(row * n_tiles, 8), n_tiles)], mask_rows, mask_sem
    )

    @pl.when(row >= col)
    def _():
        mask_copy.start()
        for copy in copies["right"] + copies["left"]:
            copy.start()
        tile = lax.broadcasted_iota(jnp.int32, (all_tiles, cols), 0)
        wanted = col * n_tiles + lax.broadcasted_iota(jnp.int32, (all_tiles, cols), 1) // MT
        pick = (tile == wanted).astype(jnp.bfloat16)
        mask_copy.wait()
        mask[...] = jnp.dot(
            mask_rows[...].astype(jnp.float32).astype(jnp.bfloat16),
            pick,
            preferred_element_type=jnp.float32,
        )

        for panel, full, high, low in (
            ("right", right, right_hi, right_lo),
            ("left", left, left_hi, left_lo),
        ):
            for copy in copies[panel]:
                copy.wait()
            rounded = full[...].astype(jnp.bfloat16)
            high[...] = rounded
            low[...] = (full[...] - rounded.astype(jnp.float32)).astype(jnp.bfloat16)

        def dot(a, b):
            return lax.dot_general(
                a, b, (((0,), (0,)), ((), ())), preferred_element_type=jnp.float32
            )

        for i in range(n_stripes):
            part = slice(i * STRIPE, (i + 1) * STRIPE)
            total = (
                dot(left_hi[:, part], right_lo[...]) + dot(left_lo[:, part], right_hi[...])
            ) + dot(left_hi[:, part], right_hi[...])
            for t in range(STRIPE // MT):
                tile = i * (STRIPE // MT) + t
                product[i, t * MT : (t + 1) * MT, :] = (
                    total[t * MT : (t + 1) * MT] * mask[tile : tile + 1, :]
                )
            store(i).start()

    for i in range(n_stripes):
        store(i).wait()


def local(inverse_rows, tile_mask):
    row = lax.axis_index("row")
    col = lax.axis_index("col")
    z, xh = row // 2, row % 2
    m, core = col // 2, col % 2
    cols = inverse_rows.shape[1]
    n = inverse_rows.shape[0]
    depth = n * 2 * NZ
    cat = lambda *parts: jnp.concatenate(parts)

    own = inverse_rows
    spread = into_plane(own)
    own_pair = cat(own, other_core(after(own, own)))
    a1 = along_z(own_pair)
    partner = other_xh(after(own, own))
    mine = to_rows(spread)
    a2 = along_z(after(a1, mine))
    b1 = other_xh(after(a1, a1))
    copies = jnp.broadcast_to(after(mine, mine)[None], (NM, n, cols))
    groups = [[2 * line + k for line in range(NM)] for k in range(2)]
    lines = lax.all_to_all(
        copies, "col", split_axis=0, concat_axis=0, tiled=True, axis_index_groups=groups
    ).reshape(NM * n, cols)
    a1x = other_core(a1)
    b1x = other_core(b1)
    b2 = along_z(after(b1, a2, a1x))
    a3 = along_z(after(a2, a2))
    a2x = other_core(a2)
    b2x = other_core(b2)
    a4 = along_z(after(a3, b2, a2x, b1x)[:n])
    b3 = along_z(after(b2, a3, b2x))
    b4 = along_z(after(b3, a4)[:n])
    a3x = other_core(a3)
    b3x = other_core(b3)
    swapped_lines = other_core(after(lines, a4, b3, partner))
    right = Pieces()
    right.add(own, (0, n, (0, 0), 0))
    right.add(partner, (0, n, (0, 1), 0))
    for steps, a, b, ax, bx in ((1, a1, b1, a1x, b1x), (2, a2, b2, a2x, b2x), (3, a3, b3, a3x, b3x)):
        right.add(a, (0, n, (steps, 0), 0))
        right.add(b, (0, n, (steps, 1), 0))
        right.add(ax, (n, n, (-steps, 0), 0))
        right.add(bx, (n, n, (-steps, 1), 0))
    right.add(a4, (0, n, (4, 0), 0))
    right.add(b4, (0, n, (4, 1), 0))

    left = Pieces()
    left.add(lines, *[(line * n, n, (line, 0), 0) for line in range(NM)])
    left.add(swapped_lines, *[(line * n, n, (line, 1), 0) for line in range(NM)])

    moves = [("right", *move) for move in right.moves]
    moves += [("left", move[0] + len(right.arrays), *move[1:]) for move in left.moves]
    arrays = [
        pltpu.with_memory_space_constraint(a, pltpu.HBM) for a in right.arrays + left.arrays
    ]
    where = jnp.stack([z, xh, m, core]).astype(jnp.int32)
    return pl.pallas_call(
        functools.partial(kernel, moves, len(arrays)),
        out_shape=jax.ShapeDtypeStruct((cols, cols), jnp.float32),
        in_specs=[
            pl.BlockSpec(memory_space=pltpu.SMEM),
            pl.BlockSpec(memory_space=pltpu.HBM),
        ]
        + [pl.BlockSpec(memory_space=pltpu.HBM)] * len(arrays),
        out_specs=pl.BlockSpec(memory_space=pltpu.HBM),
        scratch_shapes=[
            pltpu.VMEM((depth, cols), jnp.float32),
            pltpu.VMEM((depth, cols), jnp.float32),
            pltpu.VMEM((depth, cols), jnp.bfloat16),
            pltpu.VMEM((depth, cols), jnp.bfloat16),
            pltpu.VMEM((depth, cols), jnp.bfloat16),
            pltpu.VMEM((depth, cols), jnp.bfloat16),
            pltpu.VMEM((cols // STRIPE, STRIPE, cols), jnp.float32),
            pltpu.VMEM((cols // MT, cols), jnp.float32),
            pltpu.VMEM((cols // MT, tile_mask.shape[1]), jnp.int32),
            pltpu.SemaphoreType.DMA((len(moves),)),
            pltpu.SemaphoreType.DMA,
            pltpu.SemaphoreType.DMA((cols // STRIPE,)),
        ],
        compiler_params=pltpu.CompilerParams(vmem_limit_bytes=32 * 1024 * 1024),
    )(where, pltpu.with_memory_space_constraint(tile_mask, pltpu.HBM), *arrays)


def solution(mesh):
    return jax.shard_map(
        local,
        mesh=mesh,
        in_specs=(P("row", "col"), P()),
        out_specs=P("row", "col"),
        check_vma=False,
    )
```

```python
import functools

import jax
import jax.numpy as jnp
from jax import lax
from jax.experimental import pallas as pl
from jax.experimental.pallas import tpu as pltpu
from jax.sharding import PartitionSpec as P

MT = 64
AXES = ("row", "col")
NZ = 8
NM = 8
STRIPE = 256
WINDOW = 4


def permute(value, move):
    pairs = []
    for row in range(2 * NZ):
        for col in range(2 * NM):
            xh, m, z, core = move(row % 2, col // 2, row // 2, col % 2)
            pairs.append(
                (row * 2 * NM + col, (z % NZ * 2 + xh) * 2 * NM + m % NM * 2 + core)
            )
    return lax.ppermute(value, AXES, pairs)


def along_z(value):
    return permute(value, lambda xh, m, z, core: (xh, m, z + 1 - 2 * core, core))


def along_z_across(value):
    return permute(value, lambda xh, m, z, core: (1 - xh, m, z + 1 - 2 * core, core))


def along_y(value):
    return permute(value, lambda xh, m, z, core: (xh, m + 2 - 4 * core, z, core))


def into_plane(value):
    return permute(value, lambda xh, m, z, core: (core, m + z + 4 * xh, z, xh))


def to_rows(value):
    return permute(value, lambda xh, m, z, core: (xh, m, m - z + 4 * core, core))


def other_core(value):
    return permute(value, lambda xh, m, z, core: (xh, m, z, 1 - core))


def other_xh(value):
    return permute(value, lambda xh, m, z, core: (1 - xh, m, z, core))


def other_xl(value):
    return permute(value, lambda xh, m, z, core: (xh, m ^ 1, z, core))


class Steps:
    def __init__(self, window):
        self.window = window
        self.results = []

    def __call__(self, move, value):
        if len(self.results) >= self.window:
            value, _ = lax.optimization_barrier((value, self.results[-self.window]))
        self.results.append(move(value))
        return self.results[-1]


def after(value, *others):
    return lax.optimization_barrier((value, *others))[0]


class Pieces:
    def __init__(self):
        self.arrays = []
        self.moves = []

    def add(self, array, *moves):
        index = len(self.arrays)
        self.arrays.append(array)
        self.moves += [(index, *move) for move in moves]


def kernel(moves, n_in, where, mask_in, *refs):
    ins = refs[:n_in]
    out_ref = refs[n_in]
    left, right, left_hi, left_lo, right_hi, right_lo, product, mask, mask_rows, sems, mask_sem, out_sems = refs[
        n_in + 1 :
    ]
    z, xh, m, core = where[0], where[1], where[2], where[3]
    row = z * 2 + xh
    col = m * 2 + core
    sign = 1 - 2 * core
    cols = right_hi.shape[1]
    n_tiles = cols // MT
    all_tiles = mask_in.shape[0]

    def right_slot(key):
        steps, flip = key
        zz = lax.rem(z - sign * steps + 2 * NZ, NZ)
        return zz * 2 + (1 - xh if flip else xh)

    def left_slot(key):
        line, swap = key
        kappa = 1 - core if swap else core
        return lax.rem(line - z + 4 * kappa + NZ, NZ) * 2 + kappa

    copies = {"right": [], "left": []}
    for panel, index, first, count, key, offset in moves:
        buf, slot = (right, right_slot(key)) if panel == "right" else (left, left_slot(key))
        start = pl.multiple_of(slot * 64 + offset, 8)
        total = len(copies["right"]) + len(copies["left"])
        copies[panel].append(
            pltpu.make_async_copy(
                ins[index].at[pl.ds(first, count)], buf.at[pl.ds(start, count)], sems.at[total]
            )
        )
    n_stripes = out_ref.shape[0] // STRIPE

    def store(i):
        return pltpu.make_async_copy(
            product.at[i], out_ref.at[pl.ds(i * STRIPE, STRIPE)], out_sems.at[i]
        )

    @pl.when(row < col)
    def _():
        for i in range(n_stripes):
            product[i] = jnp.zeros_like(product[i])
            store(i).start()

    mask_copy = pltpu.make_async_copy(
        mask_in.at[pl.ds(pl.multiple_of(row * n_tiles, 8), n_tiles)], mask_rows, mask_sem
    )

    @pl.when(row >= col)
    def _():
        mask_copy.start()
        for copy in copies["right"] + copies["left"]:
            copy.start()
        tile = lax.broadcasted_iota(jnp.int32, (all_tiles, cols), 0)
        wanted = col * n_tiles + lax.broadcasted_iota(jnp.int32, (all_tiles, cols), 1) // MT
        pick = (tile == wanted).astype(jnp.bfloat16)
        mask_copy.wait()
        mask[...] = jnp.dot(
            mask_rows[...].astype(jnp.float32).astype(jnp.bfloat16),
            pick,
            preferred_element_type=jnp.float32,
        )

        for panel, full, high, low in (
            ("right", right, right_hi, right_lo),
            ("left", left, left_hi, left_lo),
        ):
            for copy in copies[panel]:
                copy.wait()
            rounded = full[...].astype(jnp.bfloat16)
            high[...] = rounded
            low[...] = (full[...] - rounded.astype(jnp.float32)).astype(jnp.bfloat16)

        def dot(a, b):
            return lax.dot_general(
                a, b, (((0,), (0,)), ((), ())), preferred_element_type=jnp.float32
            )

        for i in range(n_stripes):
            part = slice(i * STRIPE, (i + 1) * STRIPE)
            total = (
                dot(left_hi[:, part], right_lo[...]) + dot(left_lo[:, part], right_hi[...])
            ) + dot(left_hi[:, part], right_hi[...])
            for t in range(STRIPE // MT):
                tile = i * (STRIPE // MT) + t
                product[i, t * MT : (t + 1) * MT, :] = (
                    total[t * MT : (t + 1) * MT] * mask[tile : tile + 1, :]
                )
            store(i).start()

    for i in range(n_stripes):
        store(i).wait()


def local(inverse_rows, tile_mask):
    row = lax.axis_index("row")
    col = lax.axis_index("col")
    z, xh = row // 2, row % 2
    m, core = col // 2, col % 2
    cols = inverse_rows.shape[1]
    n = inverse_rows.shape[0]
    depth = n * 2 * NZ
    cat = lambda *parts: jnp.concatenate(parts)

    own = inverse_rows
    spread = into_plane(own)
    own_pair = cat(own, other_core(after(own, own)))
    a1 = along_z(own_pair)
    partner = other_xh(after(own, own))
    mine = to_rows(spread)
    a2 = along_z(after(a1, mine))
    b1 = other_xh(after(a1, a1))
    copies = jnp.broadcast_to(after(mine, mine)[None], (NM, n, cols))
    groups = [[2 * line + k for line in range(NM)] for k in range(2)]
    lines = lax.all_to_all(
        copies, "col", split_axis=0, concat_axis=0, tiled=True, axis_index_groups=groups
    ).reshape(NM * n, cols)
    a1x = other_core(a1)
    b1x = other_core(b1)
    b2 = along_z(after(b1, a2, a1x))
    a3 = along_z(after(a2, a2))
    a2x = other_core(a2)
    b2x = other_core(b2)
    a4 = along_z(after(a3, b2, a2x, b1x)[:n])
    b3 = along_z(after(b2, a3, b2x))
    b4 = along_z(after(b3, a4)[:n])
    a3x = other_core(a3)
    b3x = other_core(b3)
    swapped_lines = other_core(after(lines, a4, b3, partner))
    right = Pieces()
    right.add(own, (0, n, (0, 0), 0))
    right.add(partner, (0, n, (0, 1), 0))
    for steps, a, b, ax, bx in ((1, a1, b1, a1x, b1x), (2, a2, b2, a2x, b2x), (3, a3, b3, a3x, b3x)):
        right.add(a, (0, n, (steps, 0), 0))
        right.add(b, (0, n, (steps, 1), 0))
        right.add(ax, (n, n, (-steps, 0), 0))
        right.add(bx, (n, n, (-steps, 1), 0))
    right.add(a4, (0, n, (4, 0), 0))
    right.add(b4, (0, n, (4, 1), 0))

    left = Pieces()
    left.add(lines, *[(line * n, n, (line, 0), 0) for line in range(NM)])
    left.add(swapped_lines, *[(line * n, n, (line, 1), 0) for line in range(NM)])

    moves = [("right", *move) for move in right.moves]
    moves += [("left", move[0] + len(right.arrays), *move[1:]) for move in left.moves]
    arrays = [
        pltpu.with_memory_space_constraint(a, pltpu.HBM) for a in right.arrays + left.arrays
    ]
    where = jnp.stack([z, xh, m, core]).astype(jnp.int32)
    return pl.pallas_call(
        functools.partial(kernel, moves, len(arrays)),
        out_shape=jax.ShapeDtypeStruct((cols, cols), jnp.float32),
        in_specs=[
            pl.BlockSpec(memory_space=pltpu.SMEM),
            pl.BlockSpec(memory_space=pltpu.HBM),
        ]
        + [pl.BlockSpec(memory_space=pltpu.HBM)] * len(arrays),
        out_specs=pl.BlockSpec(memory_space=pltpu.HBM),
        scratch_shapes=[
            pltpu.VMEM((depth, cols), jnp.float32),
            pltpu.VMEM((depth, cols), jnp.float32),
            pltpu.VMEM((depth, cols), jnp.bfloat16),
            pltpu.VMEM((depth, cols), jnp.bfloat16),
            pltpu.VMEM((depth, cols), jnp.bfloat16),
            pltpu.VMEM((depth, cols), jnp.bfloat16),
            pltpu.VMEM((cols // STRIPE, STRIPE, cols), jnp.float32),
            pltpu.VMEM((cols // MT, cols), jnp.float32),
            pltpu.VMEM((cols // MT, tile_mask.shape[1]), jnp.int32),
            pltpu.SemaphoreType.DMA((len(moves),)),
            pltpu.SemaphoreType.DMA,
            pltpu.SemaphoreType.DMA((cols // STRIPE,)),
        ],
        compiler_params=pltpu.CompilerParams(vmem_limit_bytes=26 * 1024 * 1024),
    )(where, pltpu.with_memory_space_constraint(tile_mask, pltpu.HBM), *arrays)


def solution(mesh):
    return jax.shard_map(
        local,
        mesh=mesh,
        in_specs=(P("row", "col"), P()),
        out_specs=P("row", "col"),
        check_vma=False,
    )
```
